32 devices in a mesh: groups: 2 (over x), ctx: 16 (over z, y, core).
Axes of the slice: x: 2, y: 2, z: 4, core: 2. Of those that a mesh axis runs over, the one named last changes fastest.
Arguments:
- hidden_in: bfloat16 [32, 8192], P('groups', 'ctx'), parts along dimension 0, may hold values from -6 to 6
- attn_gain: float32 [8192], replicated, may hold values from 0.1 to 1.9
- w_query: bfloat16 [8192, 4096], P(None, 'ctx'), may hold values from -0.0625 to 0.0625
- w_key: bfloat16 [8192, 512], P(None, 'ctx'), may hold values from -0.375 to 0.375
- w_value: bfloat16 [8192, 512], P(None, 'ctx'), may hold values from -0.0625 to 0.0625
- rotated_prefix_keys: bfloat16 [32768, 4, 128], P(('groups', 'ctx')), parts along dimension 0, may hold values from -70 to 70
- cache_values: bfloat16 [32768, 4, 128], P(('groups', 'ctx')), parts along dimension 0, may hold values from -6 to 6
- w_out: bfloat16 [4096, 8192], P(None, 'ctx'), may hold values from -0.09375 to 0.09375
- ffn_gain: float32 [8192], replicated, may hold values from 0.1 to 1.9
- w_gate: bfloat16 [8192, 14336], P(None, 'ctx'), may hold values from -0.0625 to 0.0625
- w_up: bfloat16 [8192, 14336], P(None, 'ctx'), may hold values from -0.0625 to 0.0625
- w_down: bfloat16 [14336, 8192], P(None, 'ctx'), may hold values from -0.046875 to 0.046875
- doc_offsets: int32 [32], P('groups'), parts along dimension 0, may hold values from 8192 to 16384
- slot_request: int32 [32], P('groups'), parts along dimension 0, may hold values from 0 to 15, each once
Outputs:
- layer_out: bfloat16 [32, 8192], P('groups', 'ctx'), parts along dimension 0
The draws below stay inside these ranges and needn't reach their ends.
There are 2 independent parts, one for each index of `groups`. The reference program is written for one: setup_inputs(seed, part) draws one part's arguments, and reference() takes and returns one part's arrays. A program takes and returns all parts, laid end to end along the dimension named above; an argument that names none is the same for every part. Nothing has to cross between parts.
Inputs may be any that keep to these rules, and one draw needn't show every extreme that they name: `slot_request`: each slot holds a different request.
All inputs are finite; a program needn't handle non-finite values.
Results may differ from the reference program's by a relative error of at most 0.011.
Values may be sent and summed in bfloat16 or wider, within the bound.
A program may use at most 128 MiB of HBM per device.

```python
import jax
import jax.numpy as jnp
from jax import lax

D = 8192
H = 32
KVH = 4
DH = 128
FF = 14336
Q = 16
CTX_DEV = 1024
CTX = 16384


def draw_rotated_prefix_keys(key, part):
    base_key = jax.random.fold_in(jax.random.fold_in(key, 17), 0)
    shape_full = (CTX, KVH, DH)
    drawn = jnp.clip(3.0 * jax.random.normal(base_key, shape_full, jnp.float32), -24.0, 24.0)
    return drawn.astype(jnp.bfloat16)


def touch_ends(result, rng, smallest, largest):
    place = [jax.random.randint(jax.random.fold_in(rng, axis), (), 0, length) for axis, length in enumerate(result.shape)]
    widest = result.shape.index(max(result.shape))
    neighbour = place[:widest] + [(place[widest] + 1) % result.shape[widest]] + place[widest + 1:]
    return result.at[tuple(place)].set(smallest).at[tuple(neighbour)].set(largest)


def steps_of(rng, dims, pieces, least, high):
    def one(dim, shards_of):
        draws = jax.random.uniform(jax.random.fold_in(jax.random.fold_in(rng, 6), dim), (shards_of,), jnp.float32, least / len(pieces), high / len(pieces))
        return jnp.repeat(jnp.exp(draws), dims[dim] // shards_of).reshape((-1,) + (1,) * (len(dims) - dim - 1))

    loudness = one(*pieces[0])
    for cut in pieces[1:]:
        loudness = loudness * one(*cut)
    return loudness


def normal_values(rng, shape, scale, limit, pieces=(), held_as=jnp.bfloat16):
    values = scale * jax.random.normal(rng, shape, jnp.float32)
    if pieces:
        values = values * steps_of(rng, shape, pieces, -0.22, 0.18)
    return jnp.clip(values, -limit, limit).astype(held_as)


def setup_inputs(seed: int = 0, part: int = 0) -> dict:
    arg_keys = jax.random.split(jax.random.key(seed), 15)
    part_keys = jax.random.split(jax.random.fold_in(arg_keys[14], part), 15)
    hidden_in = normal_values(part_keys[0], (Q, D), 1.0, 6.0, ((1, 16),))
    attn_gain = jnp.clip(1.0 + 0.18 * jax.random.normal(arg_keys[1], (D,), jnp.float32), 0.1, 1.9)
    w_query = normal_values(arg_keys[2], (D, H * DH), D ** -0.5, 0.0625, ((1, 16),))
    w_key = normal_values(arg_keys[3], (D, KVH * DH), (D // 36) ** -0.5, 0.375, ((1, 16),))
    w_value = normal_values(arg_keys[4], (D, KVH * DH), D ** -0.5, 0.0625, ((1, 16),))
    rotated_prefix_keys = draw_rotated_prefix_keys(jax.random.fold_in(jax.random.fold_in(arg_keys[14], part), 71), part)
    cache_values = normal_values(part_keys[6], (CTX, KVH, DH), 1.0, 6.0, ((0, 16),))
    w_out = normal_values(arg_keys[7], (H * DH, D), (H * DH) ** -0.5, 0.09375, ((1, 16),))
    ffn_gain = jnp.clip(1.0 + 0.18 * jax.random.normal(arg_keys[8], (D,), jnp.float32), 0.1, 1.9)
    w_gate = normal_values(arg_keys[9], (D, FF), D ** -0.5, 0.0625, ((1, 16),))
    w_up = normal_values(arg_keys[10], (D, FF), D ** -0.5, 0.0625, ((1, 16),))
    w_down = normal_values(arg_keys[11], (FF, D), FF ** -0.5, 0.046875, ((1, 16),))
    doc_offsets = touch_ends(jax.random.randint(part_keys[12], (Q,), CTX // 2, CTX + 1), jax.random.fold_in(part_keys[12], 1), CTX // 2, CTX).astype(jnp.int32)
    slot_request = jax.random.permutation(part_keys[13], Q).astype(jnp.int32)
    return {"hidden_in": hidden_in, "attn_gain": attn_gain, "w_query": w_query, "w_key": w_key, "w_value": w_value, "rotated_prefix_keys": rotated_prefix_keys, "cache_values": cache_values, "w_out": w_out, "ffn_gain": ffn_gain, "w_gate": w_gate, "w_up": w_up, "w_down": w_down, "doc_offsets": doc_offsets, "slot_request": slot_request}


NORM_EPSILON = 1e-05
ROPE_BASE = 500000.0
MASKED = -1e+30

def rms_norm(values, gain_row):
    wide_rows = values.astype(jnp.float32)
    factor = lax.rsqrt(lax.optimization_barrier(jnp.mean(wide_rows * wide_rows, axis=1, keepdims=True)) + NORM_EPSILON)
    return (wide_rows * factor * gain_row[None, :]).astype(jnp.bfloat16)

def rotate(columns, first_col, positions, head_dim):
    col_count = columns.shape[1]
    pair_cols = first_col + jnp.arange(col_count // 2, dtype=jnp.int32) * 2
    in_head = (pair_cols % head_dim).astype(jnp.float32)
    frequency = jnp.exp(-(in_head / head_dim) * jnp.log(jnp.float32(ROPE_BASE)))
    angles = positions.astype(jnp.float32)[:, None] * frequency[None, :]
    paired = columns.reshape(columns.shape[0], col_count // 2, 2)
    even_part = paired[..., 0]
    odd_part = paired[..., 1]
    cosine = jnp.cos(angles)
    sine = jnp.sin(angles)
    turned = jnp.stack([even_part * cosine - odd_part * sine, even_part * sine + odd_part * cosine], axis=-1)
    return turned.reshape(columns.shape)

def reference(hidden_in, attn_gain, w_query, w_key, w_value, rotated_prefix_keys, cache_values, w_out, ffn_gain, w_gate, w_up, w_down, doc_offsets, slot_request):
    batch_rows = hidden_in.shape[0]
    group_size = H // KVH
    logit_scale_factor = 1.0 / DH ** 0.5
    slot_index = jnp.arange(batch_rows, dtype=jnp.int32)
    positions = lax.optimization_barrier(jnp.sum(jnp.where(slot_request[:, None] == slot_index[None, :], doc_offsets[None, :], 0), axis=1)).astype(jnp.int32)
    normed = rms_norm(hidden_in, attn_gain)
    zero_col = jnp.int32(0)
    queries = rotate(jnp.dot(normed, w_query, preferred_element_type=jnp.float32), zero_col, positions, DH).astype(jnp.bfloat16)
    key_new = rotate(jnp.dot(normed, w_key, preferred_element_type=jnp.float32), zero_col, positions, DH).astype(jnp.bfloat16)
    value_new = jnp.dot(normed, w_value, preferred_element_type=jnp.float32).astype(jnp.bfloat16)
    query_groups = queries.astype(jnp.float32).reshape(batch_rows, KVH, group_size, DH)
    block_count = CTX // CTX_DEV
    keys_blocks = rotated_prefix_keys.reshape(block_count, CTX_DEV, KVH, DH)
    values_blocks = cache_values.reshape(block_count, CTX_DEV, KVH, DH)

    def visit(running, inputs):
        run_top, run_total, run_accum = running
        block_index, prefix_block_keys, prefix_block_values = inputs
        attention_logits = jnp.einsum('owqa,zwa->owqz', query_groups, prefix_block_keys.astype(jnp.float32)) * logit_scale_factor
        places = block_index * CTX_DEV + jnp.arange(CTX_DEV, dtype=jnp.int32)
        visible = (places[None, :] < positions[:, None])[:, None, None, :]
        masked = jnp.where(visible, attention_logits, MASKED)
        block_top = lax.optimization_barrier(jnp.max(masked, axis=3))
        weights = jnp.where(visible, jnp.exp(masked - block_top[..., None]), 0.0)
        block_total = lax.optimization_barrier(jnp.sum(weights, axis=3))
        rounded_attention_weights = lax.optimization_barrier(weights.astype(jnp.bfloat16))
        block_value_sum = jnp.einsum('nelw,weh->nelh', rounded_attention_weights.astype(jnp.float32), prefix_block_values.astype(jnp.float32))
        peak_score = jnp.maximum(run_top, block_top)
        old_share = jnp.exp(run_top - peak_score)
        new_share = jnp.exp(block_top - peak_score)
        merged_total = run_total * old_share + block_total * new_share
        merged_accum = run_accum * old_share[..., None] + block_value_sum * new_share[..., None]
        return ((peak_score, merged_total, merged_accum), None)
    start_state = (jnp.full((batch_rows, KVH, group_size), MASKED, jnp.float32), jnp.zeros((batch_rows, KVH, group_size), jnp.float32), jnp.zeros((batch_rows, KVH, group_size, DH), jnp.float32))
    (global_top, global_total, prefix_accum), _ = lax.scan(visit, start_state, (jnp.arange(block_count, dtype=jnp.int32), keys_blocks, values_blocks))
    own_score = jnp.einsum('rkgd,rkd->rkg', query_groups, key_new.astype(jnp.float32).reshape(batch_rows, KVH, DH)) * logit_scale_factor
    peak_score = jnp.maximum(global_top, own_score)
    kept_share = jnp.exp(global_top - peak_score)
    fresh_share = jnp.exp(own_score - peak_score)
    denominator = global_total * kept_share + fresh_share
    spread_value = value_new.astype(jnp.float32).reshape(batch_rows, KVH, 1, DH)
    attn_rows = (prefix_accum * kept_share[..., None] + fresh_share[..., None] * spread_value) / denominator[..., None]
    attn_rows = attn_rows.reshape(batch_rows, H * DH).astype(jnp.bfloat16)
    attn_full = jnp.dot(attn_rows, w_out, preferred_element_type=jnp.float32)
    residual_mid = (hidden_in.astype(jnp.float32) + attn_full).astype(jnp.bfloat16)
    normed_mid = rms_norm(residual_mid, ffn_gain)
    gate_act = jnp.dot(normed_mid, w_gate, preferred_element_type=jnp.float32)
    up_act = jnp.dot(normed_mid, w_up, preferred_element_type=jnp.float32)
    hidden = (jax.nn.silu(gate_act) * up_act).astype(jnp.bfloat16)
    layer_out = (residual_mid.astype(jnp.float32) + jnp.dot(hidden, w_down, preferred_element_type=jnp.float32)).astype(jnp.bfloat16)
    return layer_out
```

```python
import functools
import math

import jax
import jax.numpy as jnp
from jax import lax
from jax.experimental import pallas as pl
from jax.experimental.pallas import tpu as pltpu
from jax.sharding import PartitionSpec as P

NORM_EPSILON = 1e-05
ROPE_BASE = 500000.0
MASKED = -1e30


def joined(part, axis, combine):
    gathered = jax.tree.map(lambda a: lax.all_gather(a, axis), part)

    def take(source):
        return jax.tree.map(lambda a: lax.dynamic_index_in_dim(a, source, 0, False), gathered)

    return lax.fori_loop(
        1, lax.axis_size(axis), lambda source, state: combine(state, take(source)), take(0)
    )


def rms_norm(values, gain_row):
    wide_rows = values.astype(jnp.float32)
    factor = lax.rsqrt(jnp.mean(wide_rows * wide_rows, axis=1, keepdims=True) + NORM_EPSILON)
    return (wide_rows * factor * gain_row[None, :]).astype(jnp.bfloat16)


def rotate(columns, first_col, positions, head_dim):
    col_count = columns.shape[1]
    pair_cols = first_col + jnp.arange(col_count // 2, dtype=jnp.int32) * 2
    in_head = (pair_cols % head_dim).astype(jnp.float32)
    frequency = jnp.exp(-(in_head / head_dim) * jnp.log(jnp.float32(ROPE_BASE)))
    angles = positions.astype(jnp.float32)[:, None] * frequency[None, :]
    paired = columns.reshape(columns.shape[0], col_count // 2, 2)
    even_part = paired[..., 0]
    odd_part = paired[..., 1]
    cosine = jnp.cos(angles)
    sine = jnp.sin(angles)
    turned = jnp.stack(
        [even_part * cosine - odd_part * sine, even_part * sine + odd_part * cosine], axis=-1
    )
    return turned.reshape(columns.shape)


def combine_parts(first_part, second_part):
    top_first, total_first, accum_first = first_part
    top_second, total_second, accum_second = second_part
    peak_score = jnp.maximum(top_first, top_second)
    share_first = jnp.exp(top_first - peak_score)
    share_second = jnp.exp(top_second - peak_score)
    merged_total = total_first * share_first + total_second * share_second
    merged_accum = accum_first * share_first[..., None] + accum_second * share_second[..., None]
    return (peak_score, merged_total, merged_accum)


def plain_shards(
    hidden_in,
    attn_gain,
    w_query,
    w_key,
    w_value,
    rotated_prefix_keys,
    cache_values,
    w_out,
    ffn_gain,
    w_gate,
    w_up,
    w_down,
    doc_offsets,
    slot_request,
):
    devices = lax.axis_size("ctx")
    device = lax.axis_index("ctx")
    batch_rows = hidden_in.shape[0]
    block_span, value_heads, head_dim = rotated_prefix_keys.shape
    query_width = w_query.shape[1]
    key_width = w_key.shape[1]
    head_count = query_width * devices // head_dim
    group_size = head_count // value_heads
    logit_scale_factor = 1.0 / math.sqrt(head_dim)
    slot_index = jnp.arange(batch_rows, dtype=jnp.int32)
    positions = jnp.sum(
        jnp.where(slot_request[:, None] == slot_index[None, :], doc_offsets[None, :], 0), axis=1
    )
    full_rows = lax.all_gather(hidden_in, "ctx", axis=1, tiled=True)
    normed = rms_norm(full_rows, attn_gain)
    query_part = rotate(
        jnp.dot(normed, w_query, preferred_element_type=jnp.float32),
        device * query_width,
        positions,
        head_dim,
    ).astype(jnp.bfloat16)
    key_part = rotate(
        jnp.dot(normed, w_key, preferred_element_type=jnp.float32),
        device * key_width,
        positions,
        head_dim,
    ).astype(jnp.bfloat16)
    value_part = jnp.dot(normed, w_value, preferred_element_type=jnp.float32).astype(jnp.bfloat16)
    queries, key_new, value_new = (
        lax.all_gather(query_part, "ctx", axis=1, tiled=True),
        lax.all_gather(key_part, "ctx", axis=1, tiled=True),
        lax.all_gather(value_part, "ctx", axis=1, tiled=True),
    )
    query_groups = queries.reshape(batch_rows, value_heads, group_size, head_dim)
    attention_logits = (
        jnp.einsum(
            "owqa,zwa->owqz", query_groups, rotated_prefix_keys, preferred_element_type=jnp.float32
        )
        * logit_scale_factor
    )
    places = device * block_span + jnp.arange(block_span, dtype=jnp.int32)
    visible = (places[None, :] < positions[:, None])[:, None, None, :]
    masked = jnp.where(visible, attention_logits, MASKED)
    block_top = jnp.max(masked, axis=3)
    weights = jnp.where(visible, jnp.exp(masked - block_top[..., None]), 0.0)
    block_total = jnp.sum(weights, axis=3)
    block_value_sum = jnp.einsum(
        "nelw,weh->nelh",
        weights.astype(jnp.bfloat16),
        cache_values,
        preferred_element_type=jnp.float32,
    )
    own_score = (
        jnp.einsum(
            "rkgd,rkd->rkg",
            query_groups,
            key_new.reshape(batch_rows, value_heads, head_dim),
            preferred_element_type=jnp.float32,
        )
        * logit_scale_factor
    ).reshape(batch_rows, head_count)
    spread_value = jnp.broadcast_to(
        value_new.reshape(batch_rows, value_heads, 1, head_dim),
        (batch_rows, value_heads, group_size, head_dim),
    ).reshape(batch_rows, head_count * head_dim)
    global_top, global_total, prefix_accum = joined(
        (block_top, block_total, block_value_sum), "ctx", combine_parts
    )
    finish_global_top = global_top
    finish_global_total = global_total
    finish_global_top = finish_global_top.reshape(batch_rows, head_count)
    finish_global_total = finish_global_total.reshape(batch_rows, head_count)
    peak_score = jnp.maximum(finish_global_top, own_score)
    kept_share = jnp.exp(finish_global_top - peak_score)
    fresh_share = jnp.exp(own_score - peak_score)
    denominator = finish_global_total * kept_share + fresh_share

    def columns(per_head):
        return jnp.repeat(per_head, head_dim, axis=1)

    value_cols = spread_value.astype(jnp.float32)
    attn_all = (
        (
            prefix_accum.reshape(batch_rows, head_count * head_dim) * columns(kept_share)
            + columns(fresh_share) * value_cols
        )
        / columns(denominator)
    ).astype(jnp.bfloat16)
    attn_part = jnp.dot(attn_all, w_out, preferred_element_type=jnp.float32)
    mid_part = (hidden_in.astype(jnp.float32) + attn_part).astype(jnp.bfloat16)
    mid_full = lax.all_gather(mid_part, "ctx", axis=1, tiled=True)
    normed_mid = rms_norm(mid_full, ffn_gain)
    gate_act = jnp.dot(normed_mid, w_gate, preferred_element_type=jnp.float32)
    up_act = jnp.dot(normed_mid, w_up, preferred_element_type=jnp.float32)
    hidden = (jax.nn.silu(gate_act) * up_act).astype(jnp.bfloat16)
    down_part = jnp.dot(
        lax.all_gather(hidden, "ctx", axis=1, tiled=True),
        w_down,
        preferred_element_type=jnp.float32,
    )
    return (mid_part.astype(jnp.float32) + down_part).astype(jnp.bfloat16)


MESH = pl.DeviceIdType.MESH
F32 = jnp.float32
BF16 = jnp.bfloat16


def dot(a, b):
    return jnp.dot(a, b, preferred_element_type=F32)


def dot_nt(a, b):
    return lax.dot_general(a, b, (((1,), (1,)), ((), ())), preferred_element_type=F32)


def turn(x, cosine, signed_sine):
    lane = lax.broadcasted_iota(jnp.int32, x.shape, 1)
    after = pltpu.roll(x, x.shape[1] - 1, 1)
    before = pltpu.roll(x, 1, 1)
    return x * cosine + jnp.where(lane % 2 == 0, after, before) * signed_sine


def three_terms(x):
    high = x.astype(BF16).astype(F32)
    left = x - high
    mid = left.astype(BF16).astype(F32)
    return high, mid, left - mid


def layer_kernel(
    n,
    hidden_ref,
    again_ref,
    fgain_ref,
    table_ref,
    place_ref,
    wq_hbm,
    wk_hbm,
    wv_hbm,
    keys_hbm,
    values_hbm,
    wo_hbm,
    wg_hbm,
    wu_hbm,
    wd_hbm,
    out_ref,
    wq,
    wkv,
    keys,
    values,
    wo,
    wg,
    wu,
    wd,
    xbuf,
    qbuf,
    asend,
    arecv,
    abuf,
    mbuf,
    hbuf,
    nbuf,
    local_sem,
    send_sem,
    recv_sem,
):
    me = lax.axis_index("ctx")
    rows = hidden_ref.shape[0]
    kv_heads, span, head_dim = keys.shape
    q_width = wq.shape[2]
    k_width = wk_hbm.shape[0]
    own_heads = q_width // head_dim
    head_count = own_heads * n
    group = head_count // kv_heads
    stat_lanes = head_dim // own_heads
    scale = 1.0 / math.sqrt(head_dim)

    loads = [
        pltpu.make_async_copy(source, target, local_sem.at[i])
        for i, (source, target) in enumerate(
            [
                (wq_hbm, wq),
                (wk_hbm, wkv.at[pl.ds(0, k_width)]),
                (wv_hbm, wkv.at[pl.ds(k_width, k_width)]),
                (keys_hbm, keys),
                (values_hbm, values),
                (wo_hbm, wo),
                (wg_hbm, wg),
                (wu_hbm, wu),
                (wd_hbm, wd),
            ]
        )
    ]
    for load in loads:
        load.start()

    barrier = pltpu.get_barrier_semaphore()

    @pl.loop(1, n)
    def _(i):
        pl.semaphore_signal(
            barrier, inc=1, device_id={"ctx": lax.rem(me + i, n)}, device_id_type=MESH
        )

    xbuf[me] = hidden_ref[...]
    pl.semaphore_wait(barrier, n - 1)

    other_core = me + 1 - 2 * (me % 2)
    other_y = me + 2 - 4 * ((me // 2) % 2)
    other_both = other_y + 1 - 2 * (other_y % 2)
    z_steps = n // 4

    def along_z(base, i):
        return lax.rem(base + 4 * i, n)

    def block_copy(buf, phase, block, target, k):
        return pltpu.make_async_remote_copy(
            src_ref=buf.at[block],
            dst_ref=buf.at[block],
            send_sem=send_sem.at[phase, k],
            recv_sem=recv_sem.at[phase, block],
            device_id={"ctx": target},
            device_id_type=MESH,
        )

    def await_block(buf, phase, block):
        block_copy(buf, phase, block, other_core, 0).wait_recv()

    def gather(buf, phase):
        for i in range(1, z_steps):
            block_copy(buf, phase, me, along_z(me, i), i - 1).start()
        k = z_steps - 1
        block_copy(buf, phase, me, other_y, k).start()
        block_copy(buf, phase, me, other_core, k + 1).start()
        k += 2
        for i in range(1, z_steps):
            block = along_z(me, n // 4 - i)
            await_block(buf, phase, block)
            block_copy(buf, phase, block, other_y, k).start()
            block_copy(buf, phase, block, other_core, k + 1).start()
            k += 2
        for i in range(z_steps):
            block = along_z(other_y, (z_steps - i) % z_steps)
            await_block(buf, phase, block)
            block_copy(buf, phase, block, other_core, k).start()
            k += 1
        for i in range(z_steps):
            await_block(buf, phase, along_z(other_core, (z_steps - i) % z_steps))
        for i in range(z_steps):
            await_block(buf, phase, along_z(other_both, (z_steps - i) % z_steps))

    def finish_sends(buf, phase):
        @pl.loop(0, n - 1)
        def _(k):
            block_copy(buf, phase, me, other_core, k).wait_send()

    def normalise(buf, gain_ref):
        width = buf.shape[2]

        def add(s, total):
            x = buf[s].astype(F32)
            return total + x * x

        squares = lax.fori_loop(0, n, add, jnp.zeros((rows, width), F32), unroll=4)
        mean = jnp.sum(squares, axis=1, keepdims=True) / (width * n)
        factor = lax.rsqrt(mean + NORM_EPSILON)

        @pl.loop(0, n, unroll=4)
        def _(s):
            nbuf[s] = (buf[s].astype(F32) * factor * gain_ref[s]).astype(BF16)

    def product(buf, weight):
        def add(s, total):
            return total + dot(buf[s], weight[s])

        return lax.fori_loop(0, n, add, jnp.zeros((rows, weight.shape[2]), F32), unroll=4)

    gather(xbuf, 0)
    normalise(xbuf, again_ref)
    loads[0].wait()
    q_part = product(nbuf, wq)
    cosine, sine = table_ref[0], table_ref[1]
    for h in range(own_heads):
        cols = slice(h * head_dim, (h + 1) * head_dim)
        qbuf[me, :, cols] = turn(q_part[:, cols], cosine, sine).astype(BF16)
    loads[1].wait()
    loads[2].wait()
    kv_part = jnp.zeros((rows, 2 * k_width), F32)
    width = nbuf.shape[2]
    for s in range(n):
        kv_part += dot_nt(nbuf[s], wkv[:, s * width : (s + 1) * width])
    kv_part = jnp.concatenate(
        [kv_part, jnp.zeros((rows, head_dim - 2 * k_width), F32)], axis=1
    )
    qbuf[me, :, q_width:] = turn(kv_part, table_ref[2], table_ref[3]).astype(BF16)
    gather(qbuf, 1)

    loads[3].wait()
    loads[4].wait()
    lane = lax.broadcasted_iota(jnp.int32, (rows, head_dim), 1)
    place = place_ref[...]
    limit = jnp.concatenate([place] * group, axis=0)[:, 0:1]
    at = me * span + lax.broadcasted_iota(jnp.int32, (group * rows, span), 1)
    visible = at < limit

    def part_copy(target, source):
        return pltpu.make_async_remote_copy(
            src_ref=asend.at[target],
            dst_ref=arecv.at[source],
            send_sem=send_sem.at[2, target],
            recv_sem=recv_sem.at[2, source],
            device_id={"ctx": target},
            device_id_type=MESH,
        )

    for g in range(kv_heads):
        query = jnp.concatenate(
            [
                qbuf[h // own_heads, :, (h % own_heads) * head_dim : (h % own_heads + 1) * head_dim]
                for h in range(g * group, (g + 1) * group)
            ],
            axis=0,
        )
        logits = jnp.where(visible, dot_nt(query, keys[g]) * scale, MASKED)
        top = jnp.max(logits, axis=1, keepdims=True)
        weights = jnp.where(visible, jnp.exp(logits - top), 0.0)
        total = jnp.sum(weights, axis=1, keepdims=True)
        accum = dot(weights.astype(BF16), values[g]).astype(BF16)
        terms = three_terms(top) + three_terms(total)
        for d in range(group // own_heads):
            target = g * (group // own_heads) + d
            stats = jnp.zeros((rows, head_dim), F32)
            for h in range(own_heads):
                j = d * own_heads + h
                these = slice(j * rows, (j + 1) * rows)
                asend[target, h * rows : (h + 1) * rows, :] = accum[these]
                for t, term in enumerate(terms):
                    stats = jnp.where(lane == h * stat_lanes + t, term[these], stats)
            asend[target, own_heads * rows :, :] = stats.astype(BF16)

            @pl.when(me != target)
            def _():
                part_copy(target, me).start()

    arecv[me] = asend[me]

    @pl.loop(1, n)
    def _(i):
        part_copy(0, lax.rem(me + i, n)).wait_recv()

    def stats_of(s):
        x = arecv[s, own_heads * rows :, :].astype(F32)
        return x + pltpu.roll(x, head_dim - 1, 1) + pltpu.roll(x, head_dim - 2, 1)

    tops = lax.fori_loop(
        1, n, lambda s, top: jnp.maximum(top, stats_of(s)), stats_of(0), unroll=5
    )

    def merge(s, state):
        stats = stats_of(s)
        share = jnp.exp(stats - tops)
        total = state[0] + pltpu.roll(stats, head_dim - 3, 1) * share
        accums = tuple(
            state[1 + h]
            + arecv[s, h * rows : (h + 1) * rows, :].astype(F32)
            * share[:, h * stat_lanes : h * stat_lanes + 1]
            for h in range(own_heads)
        )
        return (total, *accums)

    zero = jnp.zeros((rows, head_dim), F32)
    totals, *accums = lax.fori_loop(0, n, merge, (zero,) * (1 + own_heads), unroll=4)

    pieces = head_dim // k_width
    first_piece = (me * own_heads // group) * pieces
    key_new, value_new = zero, zero
    for i in range(pieces):
        piece = qbuf[first_piece + i, :, q_width:].astype(F32)
        key_piece = jnp.where(lane < k_width, piece, 0.0)
        value_piece = jnp.where((lane >= k_width) & (lane < 2 * k_width), piece, 0.0)
        key_new += pltpu.roll(key_piece, i * k_width, 1) if i else key_piece
        shift = (i * k_width - k_width) % head_dim
        value_new += pltpu.roll(value_piece, shift, 1) if shift else value_piece
    for h in range(own_heads):
        cols = slice(h * head_dim, (h + 1) * head_dim)
        at_stat = slice(h * stat_lanes, h * stat_lanes + 1)
        query = qbuf[me, :, cols].astype(F32)
        own_score = jnp.sum(query * key_new, axis=1, keepdims=True) * scale
        top = tops[:, at_stat]
        peak = jnp.maximum(top, own_score)
        kept, fresh = jnp.exp(top - peak), jnp.exp(own_score - peak)
        below = totals[:, at_stat] * kept + fresh
        abuf[me, :, cols] = ((accums[h] * kept + fresh * value_new) / below).astype(BF16)
    gather(abuf, 3)

    loads[5].wait()
    mid = (hidden_ref[...].astype(F32) + product(abuf, wo)).astype(BF16)
    mbuf[me] = mid
    gather(mbuf, 4)
    normalise(mbuf, fgain_ref)
    loads[6].wait()
    gate = product(nbuf, wg)
    loads[7].wait()
    up = product(nbuf, wu)
    hbuf[me] = (gate / (1.0 + jnp.exp(-gate)) * up).astype(BF16)
    gather(hbuf, 5)
    loads[8].wait()
    out_ref[...] = (mid.astype(F32) + product(hbuf, wd)).astype(BF16)

    finish_sends(xbuf, 0)
    finish_sends(qbuf, 1)

    @pl.loop(1, n)
    def _(i):
        part_copy(lax.rem(me + i, n), 0).wait_send()

    finish_sends(abuf, 3)
    finish_sends(mbuf, 4)
    finish_sends(hbuf, 5)


def angle_tables(positions, device, key_width, head_dim):
    lane = jnp.arange(2 * head_dim, dtype=jnp.int32)
    second = lane >= head_dim
    col = jnp.where(second, lane + device * key_width, lane) % head_dim
    frequency = jnp.exp(
        -((col - col % 2).astype(F32) / head_dim) * jnp.log(jnp.float32(ROPE_BASE))
    )
    turned = ~second | (lane < head_dim + key_width)
    angles = positions.astype(F32)[:, None] * jnp.where(turned, frequency, 0.0)[None, :]
    sign = jnp.where(lane % 2 == 0, -1.0, 1.0)
    cosine, sine = jnp.cos(angles), jnp.sin(angles) * sign[None, :]
    return jnp.stack(
        [cosine[:, :head_dim], sine[:, :head_dim], cosine[:, head_dim:], sine[:, head_dim:]]
    )


def shards(
    hidden_in,
    attn_gain,
    w_query,
    w_key,
    w_value,
    rotated_prefix_keys,
    cache_values,
    w_out,
    ffn_gain,
    w_gate,
    w_up,
    w_down,
    doc_offsets,
    slot_request,
):
    n = lax.axis_size("ctx")
    device = lax.axis_index("ctx")
    rows, width = hidden_in.shape
    span, kv_heads, head_dim = rotated_prefix_keys.shape
    q_width, k_width = w_query.shape[1], w_key.shape[1]
    ff_width = w_gate.shape[1]
    slot_index = jnp.arange(rows, dtype=jnp.int32)
    positions = jnp.sum(
        jnp.where(slot_request[:, None] == slot_index[None, :], doc_offsets[None, :], 0), axis=1
    )
    tables = angle_tables(positions, device, k_width, head_dim)
    place = jnp.broadcast_to(positions[:, None], (rows, head_dim))
    own_heads = q_width // head_dim
    vmem = pl.BlockSpec(memory_space=pltpu.VMEM)
    hbm = pl.BlockSpec(memory_space=pl.ANY)
    weight_shapes = [
        (n, width, q_width),
        (2 * k_width, width * n),
        (kv_heads, span, head_dim),
        (kv_heads, span, head_dim),
        (n, q_width, width),
        (n, width, ff_width),
        (n, width, ff_width),
        (n, ff_width, width),
    ]
    block_shapes = [
        (n, rows, width),
        (n, rows, q_width + head_dim),
        (n, (own_heads + 1) * rows, head_dim),
        (n, (own_heads + 1) * rows, head_dim),
        (n, rows, q_width),
        (n, rows, width),
        (n, rows, ff_width),
        (n, rows, width),
    ]
    return pl.pallas_call(
        functools.partial(layer_kernel, n),
        out_shape=jax.ShapeDtypeStruct((rows, width), BF16),
        in_specs=[vmem] * 5 + [hbm] * 9,
        out_specs=vmem,
        scratch_shapes=[pltpu.VMEM(shape, BF16) for shape in weight_shapes + block_shapes]
        + [
            pltpu.SemaphoreType.DMA((9,)),
            pltpu.SemaphoreType.DMA((6, n)),
            pltpu.SemaphoreType.DMA((6, n)),
        ],
        compiler_params=pltpu.CompilerParams(
            collective_id=0, has_side_effects=True, vmem_limit_bytes=62 * 1024 * 1024
        ),
        name="layer",
    )(
        hidden_in,
        attn_gain.reshape(n, 1, width),
        ffn_gain.reshape(n, 1, width),
        tables,
        place,
        w_query.reshape(n, width, q_width),
        w_key.T,
        w_value.T,
        jnp.transpose(rotated_prefix_keys, (1, 0, 2)),
        jnp.transpose(cache_values, (1, 0, 2)),
        w_out.reshape(n, q_width, width),
        w_gate.reshape(n, width, ff_width),
        w_up.reshape(n, width, ff_width),
        w_down.reshape(n, ff_width, width),
    )


def pick(*arrays):
    n = lax.axis_size("ctx")
    rows, width = arrays[0].shape
    span, kv_heads, head_dim = arrays[5].shape
    q_width, k_width, ff_width = arrays[2].shape[1], arrays[3].shape[1], arrays[9].shape[1]
    whole_tiles = (
        n % 4 == 0
        and n >= 8
        and head_dim == 128
        and rows % 16 == 0
        and all(w % 128 == 0 for w in (width, q_width, ff_width, span))
        and k_width % 16 == 0
        and 2 * k_width <= head_dim
        and head_dim % k_width == 0
    )
    if not whole_tiles:
        return plain_shards(*arrays)
    own_heads = q_width // head_dim
    group = own_heads * n // kv_heads
    if group % own_heads or own_heads > 8:
        return plain_shards(*arrays)
    return shards(*arrays)


def solution(mesh):
    return jax.shard_map(
        pick,
        mesh=mesh,
        in_specs=(
            P("groups", "ctx"),
            P(),
            P(None, "ctx"),
            P(None, "ctx"),
            P(None, "ctx"),
            P(("groups", "ctx"), None, None),
            P(("groups", "ctx"), None, None),
            P(None, "ctx"),
            P(),
            P(None, "ctx"),
            P(None, "ctx"),
            P(None, "ctx"),
            P("groups"),
            P("groups"),
        ),
        out_specs=P("groups", "ctx"),
        check_vma=False,
    )
```

```python
import functools
import math

import jax
import jax.numpy as jnp
from jax import lax
from jax.experimental import pallas as pl
from jax.experimental.pallas import tpu as pltpu
from jax.sharding import PartitionSpec as P

NORM_EPSILON = 1e-05
ROPE_BASE = 500000.0
MASKED = -1e30


def joined(part, axis, combine):
    gathered = jax.tree.map(lambda a: lax.all_gather(a, axis), part)

    def take(source):
        return jax.tree.map(lambda a: lax.dynamic_index_in_dim(a, source, 0, False), gathered)

    return lax.fori_loop(
        1, lax.axis_size(axis), lambda source, state: combine(state, take(source)), take(0)
    )


def rms_norm(values, gain_row):
    wide_rows = values.astype(jnp.float32)
    factor = lax.rsqrt(jnp.mean(wide_rows * wide_rows, axis=1, keepdims=True) + NORM_EPSILON)
    return (wide_rows * factor * gain_row[None, :]).astype(jnp.bfloat16)


def rotate(columns, first_col, positions, head_dim):
    col_count = columns.shape[1]
    pair_cols = first_col + jnp.arange(col_count // 2, dtype=jnp.int32) * 2
    in_head = (pair_cols % head_dim).astype(jnp.float32)
    frequency = jnp.exp(-(in_head / head_dim) * jnp.log(jnp.float32(ROPE_BASE)))
    angles = positions.astype(jnp.float32)[:, None] * frequency[None, :]
    paired = columns.reshape(columns.shape[0], col_count // 2, 2)
    even_part = paired[..., 0]
    odd_part = paired[..., 1]
    cosine = jnp.cos(angles)
    sine = jnp.sin(angles)
    turned = jnp.stack(
        [even_part * cosine - odd_part * sine, even_part * sine + odd_part * cosine], axis=-1
    )
    return turned.reshape(columns.shape)


def combine_parts(first_part, second_part):
    top_first, total_first, accum_first = first_part
    top_second, total_second, accum_second = second_part
    peak_score = jnp.maximum(top_first, top_second)
    share_first = jnp.exp(top_first - peak_score)
    share_second = jnp.exp(top_second - peak_score)
    merged_total = total_first * share_first + total_second * share_second
    merged_accum = accum_first * share_first[..., None] + accum_second * share_second[..., None]
    return (peak_score, merged_total, merged_accum)


def plain_shards(
    hidden_in,
    attn_gain,
    w_query,
    w_key,
    w_value,
    rotated_prefix_keys,
    cache_values,
    w_out,
    ffn_gain,
    w_gate,
    w_up,
    w_down,
    doc_offsets,
    slot_request,
):
    devices = lax.axis_size("ctx")
    device = lax.axis_index("ctx")
    batch_rows = hidden_in.shape[0]
    block_span, value_heads, head_dim = rotated_prefix_keys.shape
    query_width = w_query.shape[1]
    key_width = w_key.shape[1]
    head_count = query_width * devices // head_dim
    group_size = head_count // value_heads
    logit_scale_factor = 1.0 / math.sqrt(head_dim)
    slot_index = jnp.arange(batch_rows, dtype=jnp.int32)
    positions = jnp.sum(
        jnp.where(slot_request[:, None] == slot_index[None, :], doc_offsets[None, :], 0), axis=1
    )
    full_rows = lax.all_gather(hidden_in, "ctx", axis=1, tiled=True)
    normed = rms_norm(full_rows, attn_gain)
    query_part = rotate(
        jnp.dot(normed, w_query, preferred_element_type=jnp.float32),
        device * query_width,
        positions,
        head_dim,
    ).astype(jnp.bfloat16)
    key_part = rotate(
        jnp.dot(normed, w_key, preferred_element_type=jnp.float32),
        device * key_width,
        positions,
        head_dim,
    ).astype(jnp.bfloat16)
    value_part = jnp.dot(normed, w_value, preferred_element_type=jnp.float32).astype(jnp.bfloat16)
    queries, key_new, value_new = (
        lax.all_gather(query_part, "ctx", axis=1, tiled=True),
        lax.all_gather(key_part, "ctx", axis=1, tiled=True),
        lax.all_gather(value_part, "ctx", axis=1, tiled=True),
    )
    query_groups = queries.reshape(batch_rows, value_heads, group_size, head_dim)
    attention_logits = (
        jnp.einsum(
            "owqa,zwa->owqz", query_groups, rotated_prefix_keys, preferred_element_type=jnp.float32
        )
        * logit_scale_factor
    )
    places = device * block_span + jnp.arange(block_span, dtype=jnp.int32)
    visible = (places[None, :] < positions[:, None])[:, None, None, :]
    masked = jnp.where(visible, attention_logits, MASKED)
    block_top = jnp.max(masked, axis=3)
    weights = jnp.where(visible, jnp.exp(masked - block_top[..., None]), 0.0)
    block_total = jnp.sum(weights, axis=3)
    block_value_sum = jnp.einsum(
        "nelw,weh->nelh",
        weights.astype(jnp.bfloat16),
        cache_values,
        preferred_element_type=jnp.float32,
    )
    own_score = (
        jnp.einsum(
            "rkgd,rkd->rkg",
            query_groups,
            key_new.reshape(batch_rows, value_heads, head_dim),
            preferred_element_type=jnp.float32,
        )
        * logit_scale_factor
    ).reshape(batch_rows, head_count)
    spread_value = jnp.broadcast_to(
        value_new.reshape(batch_rows, value_heads, 1, head_dim),
        (batch_rows, value_heads, group_size, head_dim),
    ).reshape(batch_rows, head_count * head_dim)
    global_top, global_total, prefix_accum = joined(
        (block_top, block_total, block_value_sum), "ctx", combine_parts
    )
    finish_global_top = global_top
    finish_global_total = global_total
    finish_global_top = finish_global_top.reshape(batch_rows, head_count)
    finish_global_total = finish_global_total.reshape(batch_rows, head_count)
    peak_score = jnp.maximum(finish_global_top, own_score)
    kept_share = jnp.exp(finish_global_top - peak_score)
    fresh_share = jnp.exp(own_score - peak_score)
    denominator = finish_global_total * kept_share + fresh_share

    def columns(per_head):
        return jnp.repeat(per_head, head_dim, axis=1)

    value_cols = spread_value.astype(jnp.float32)
    attn_all = (
        (
            prefix_accum.reshape(batch_rows, head_count * head_dim) * columns(kept_share)
            + columns(fresh_share) * value_cols
        )
        / columns(denominator)
    ).astype(jnp.bfloat16)
    attn_part = jnp.dot(attn_all, w_out, preferred_element_type=jnp.float32)
    mid_part = (hidden_in.astype(jnp.float32) + attn_part).astype(jnp.bfloat16)
    mid_full = lax.all_gather(mid_part, "ctx", axis=1, tiled=True)
    normed_mid = rms_norm(mid_full, ffn_gain)
    gate_act = jnp.dot(normed_mid, w_gate, preferred_element_type=jnp.float32)
    up_act = jnp.dot(normed_mid, w_up, preferred_element_type=jnp.float32)
    hidden = (jax.nn.silu(gate_act) * up_act).astype(jnp.bfloat16)
    down_part = jnp.dot(
        lax.all_gather(hidden, "ctx", axis=1, tiled=True),
        w_down,
        preferred_element_type=jnp.float32,
    )
    return (mid_part.astype(jnp.float32) + down_part).astype(jnp.bfloat16)


MESH = pl.DeviceIdType.MESH
F32 = jnp.float32
BF16 = jnp.bfloat16


def dot(a, b):
    return jnp.dot(a, b, preferred_element_type=F32)


def dot_nt(a, b):
    return lax.dot_general(a, b, (((1,), (1,)), ((), ())), preferred_element_type=F32)


def turn(x, cosine, signed_sine):
    lane = lax.broadcasted_iota(jnp.int32, x.shape, 1)
    after = pltpu.roll(x, x.shape[1] - 1, 1)
    before = pltpu.roll(x, 1, 1)
    return x * cosine + jnp.where(lane % 2 == 0, after, before) * signed_sine


def three_terms(x):
    high = x.astype(BF16).astype(F32)
    left = x - high
    mid = left.astype(BF16).astype(F32)
    return high, mid, left - mid


def layer_kernel(
    n,
    hidden_ref,
    again_ref,
    fgain_ref,
    table_ref,
    place_ref,
    wq_hbm,
    wk_hbm,
    wv_hbm,
    keys_hbm,
    values_hbm,
    wo_hbm,
    wg_hbm,
    wu_hbm,
    wd_hbm,
    out_ref,
    wq,
    wkv,
    keys,
    values,
    wo,
    wg,
    wu,
    wd,
    xbuf,
    qbuf,
    asend,
    arecv,
    abuf,
    mbuf,
    hbuf,
    local_sem,
    send_sem,
    recv_sem,
):
    me = lax.axis_index("ctx")
    rows = hidden_ref.shape[0]
    kv_heads, span, head_dim = keys.shape
    q_width = wq.shape[2]
    k_width = wk_hbm.shape[0]
    own_heads = q_width // head_dim
    head_count = own_heads * n
    group = head_count // kv_heads
    stat_lanes = head_dim // own_heads
    scale = 1.0 / math.sqrt(head_dim)

    loads = [
        pltpu.make_async_copy(source, target, local_sem.at[i])
        for i, (source, target) in enumerate(
            [
                (wq_hbm, wq),
                (wk_hbm, wkv.at[pl.ds(0, k_width)]),
                (wv_hbm, wkv.at[pl.ds(k_width, k_width)]),
                (keys_hbm, keys),
                (values_hbm, values),
                (wo_hbm, wo),
                (wg_hbm, wg),
                (wu_hbm, wu),
                (wd_hbm, wd),
            ]
        )
    ]
    for load in loads:
        load.start()

    barrier = pltpu.get_barrier_semaphore()

    @pl.loop(1, n)
    def _(i):
        pl.semaphore_signal(
            barrier, inc=1, device_id={"ctx": lax.rem(me + i, n)}, device_id_type=MESH
        )

    low, z, z_steps = me % 4, me // 4, n // 4
    xbuf[low, z] = hidden_ref[...]
    pl.semaphore_wait(barrier, n - 1)

    other_core = me + 1 - 2 * (me % 2)
    other_y = me + 2 - 4 * ((me // 2) % 2)
    other_both = other_y + 1 - 2 * (other_y % 2)

    def block_copy(buf, phase, from_z, target, k):
        return pltpu.make_async_remote_copy(
            src_ref=buf.at[low, from_z],
            dst_ref=buf.at[low, from_z],
            send_sem=send_sem.at[phase, k],
            recv_sem=recv_sem.at[phase, from_z],
            device_id={"ctx": target},
            device_id_type=MESH,
        )

    def set_copy(buf, phase, which, target, k):
        return pltpu.make_async_remote_copy(
            src_ref=buf.at[which],
            dst_ref=buf.at[which],
            send_sem=send_sem.at[phase, z_steps - 1 + k],
            recv_sem=recv_sem.at[phase, z_steps + which],
            device_id={"ctx": target},
            device_id_type=MESH,
        )

    def gather(buf, phase):
        for i in range(1, z_steps):
            block_copy(buf, phase, z, lax.rem(me + 4 * i, n), i - 1).start()
        for i in range(1, z_steps):
            block_copy(buf, phase, lax.rem(z + i, z_steps), other_core, 0).wait_recv()
        for k, peer in enumerate((other_both, other_y, other_core)):
            set_copy(buf, phase, low, peer, k).start()
        yield low
        for peer in (other_core, other_y, other_both):
            which = peer % 4
            set_copy(buf, phase, which, other_core, 0).wait_recv()
            yield which

    def gather_all(buf, phase):
        for _ in gather(buf, phase):
            pass

    def finish_sends(buf, phase):
        for i in range(1, z_steps):
            block_copy(buf, phase, z, other_core, i - 1).wait_send()
        for k in range(3):
            set_copy(buf, phase, low, other_core, k).wait_send()

    def over_set(step, which, state):
        return lax.fori_loop(
            0, z_steps, lambda at_z, state: step(which, at_z, at_z * 4 + which, state), state,
            unroll=True,
        )

    def row_factor(squares):
        mean = jnp.sum(squares, axis=1, keepdims=True) / (squares.shape[1] * n)
        return lax.rsqrt(mean + NORM_EPSILON)

    def product(buf, phase, load, weight):
        def add(which, at_z, source, total):
            return total + dot(buf[which, at_z], weight[source])

        total = jnp.zeros((rows, weight.shape[2]), F32)
        for step, which in enumerate(gather(buf, phase)):
            if step == 0:
                load.wait()
            total = over_set(add, which, total)
        return total

    width = xbuf.shape[3]

    def project_in(which, at_z, source, state):
        squares, q_part, kv_part = state
        x = xbuf[which, at_z].astype(F32)
        scaled = (x * again_ref[source]).astype(BF16)
        cols = pl.ds(pl.multiple_of(source * width, width), width)
        return (
            squares + x * x,
            q_part + dot(scaled, wq[source]),
            kv_part + dot_nt(scaled, wkv[:, cols]),
        )

    state = tuple(jnp.zeros((rows, w), F32) for w in (width, q_width, 2 * k_width))
    for step, which in enumerate(gather(xbuf, 0)):
        if step == 0:
            for load in loads[:3]:
                load.wait()
        state = over_set(project_in, which, state)
    factor = row_factor(state[0])
    q_part, kv_part = state[1] * factor, state[2] * factor
    cosine, sine = table_ref[0], table_ref[1]
    for h in range(own_heads):
        cols = slice(h * head_dim, (h + 1) * head_dim)
        qbuf[low, z, :, cols] = turn(q_part[:, cols], cosine, sine).astype(BF16)
    kv_part = jnp.concatenate(
        [kv_part, jnp.zeros((rows, head_dim - 2 * k_width), F32)], axis=1
    )
    qbuf[low, z, :, q_width:] = turn(kv_part, table_ref[2], table_ref[3]).astype(BF16)
    gather_all(qbuf, 1)

    loads[3].wait()
    loads[4].wait()
    lane = lax.broadcasted_iota(jnp.int32, (rows, head_dim), 1)
    place = place_ref[...]
    limit = jnp.concatenate([place] * group, axis=0)[:, 0:1]
    at = me * span + lax.broadcasted_iota(jnp.int32, (group * rows, span), 1)
    visible = at < limit

    def part_copy(target, source):
        return pltpu.make_async_remote_copy(
            src_ref=asend.at[target],
            dst_ref=arecv.at[source],
            send_sem=send_sem.at[2, target],
            recv_sem=recv_sem.at[2, source],
            device_id={"ctx": target},
            device_id_type=MESH,
        )

    for g in range(kv_heads):
        query = jnp.concatenate(
            [
                qbuf[d % 4, d // 4, :, h * head_dim : (h + 1) * head_dim]
                for d in range(g * group // own_heads, (g + 1) * group // own_heads)
                for h in range(own_heads)
            ],
            axis=0,
        )
        logits = jnp.where(visible, dot_nt(query, keys[g]) * scale, MASKED)
        top = jnp.max(logits, axis=1, keepdims=True)
        weights = jnp.where(visible, jnp.exp(logits - top), 0.0)
        total = jnp.sum(weights, axis=1, keepdims=True)
        accum = dot(weights.astype(BF16), values[g]).astype(BF16)
        terms = three_terms(top) + three_terms(total)
        for d in range(group // own_heads):
            target = g * (group // own_heads) + d
            stats = jnp.zeros((rows, head_dim), F32)
            for h in range(own_heads):
                j = d * own_heads + h
                these = slice(j * rows, (j + 1) * rows)
                asend[target, h * rows : (h + 1) * rows, :] = accum[these]
                for t, term in enumerate(terms):
                    stats = jnp.where(lane == h * stat_lanes + t, term[these], stats)
            asend[target, own_heads * rows :, :] = stats.astype(BF16)

            @pl.when(me != target)
            def _():
                part_copy(target, me).start()

    arecv[me] = asend[me]

    @pl.loop(1, n)
    def _(i):
        part_copy(0, lax.rem(me + i, n)).wait_recv()

    def stats_of(s):
        x = arecv[s, own_heads * rows :, :].astype(F32)
        return x + pltpu.roll(x, head_dim - 1, 1) + pltpu.roll(x, head_dim - 2, 1)

    tops = lax.fori_loop(
        1, n, lambda s, top: jnp.maximum(top, stats_of(s)), stats_of(0), unroll=5
    )

    def merge(s, state):
        stats = stats_of(s)
        share = jnp.exp(stats - tops)
        total = state[0] + pltpu.roll(stats, head_dim - 3, 1) * share
        accums = tuple(
            state[1 + h]
            + arecv[s, h * rows : (h + 1) * rows, :].astype(F32)
            * share[:, h * stat_lanes : h * stat_lanes + 1]
            for h in range(own_heads)
        )
        return (total, *accums)

    zero = jnp.zeros((rows, head_dim), F32)
    totals, *accums = lax.fori_loop(0, n, merge, (zero,) * (1 + own_heads), unroll=4)

    pieces = head_dim // k_width
    first_piece = (me * own_heads // group) * pieces
    key_new, value_new = zero, zero
    for i in range(pieces):
        source = first_piece + i
        piece = qbuf[source % 4, source // 4, :, q_width:].astype(F32)
        key_piece = jnp.where(lane < k_width, piece, 0.0)
        value_piece = jnp.where((lane >= k_width) & (lane < 2 * k_width), piece, 0.0)
        key_new += pltpu.roll(key_piece, i * k_width, 1) if i else key_piece
        shift = (i * k_width - k_width) % head_dim
        value_new += pltpu.roll(value_piece, shift, 1) if shift else value_piece
    for h in range(own_heads):
        cols = slice(h * head_dim, (h + 1) * head_dim)
        at_stat = slice(h * stat_lanes, h * stat_lanes + 1)
        query = qbuf[low, z, :, cols].astype(F32)
        own_score = jnp.sum(query * key_new, axis=1, keepdims=True) * scale
        top = tops[:, at_stat]
        peak = jnp.maximum(top, own_score)
        kept, fresh = jnp.exp(top - peak), jnp.exp(own_score - peak)
        below = totals[:, at_stat] * kept + fresh
        abuf[low, z, :, cols] = ((accums[h] * kept + fresh * value_new) / below).astype(BF16)

    attn_part = product(abuf, 3, loads[5], wo)
    mid = (hidden_ref[...].astype(F32) + attn_part).astype(BF16)
    mbuf[low, z] = mid

    def feed(which, at_z, source, state):
        squares, gate, up = state
        x = mbuf[which, at_z].astype(F32)
        scaled = (x * fgain_ref[source]).astype(BF16)
        return (
            squares + x * x,
            gate + dot(scaled, wg[source]),
            up + dot(scaled, wu[source]),
        )

    ff_width = wg.shape[2]
    state = tuple(jnp.zeros((rows, w), F32) for w in (width, ff_width, ff_width))
    for step, which in enumerate(gather(mbuf, 4)):
        if step == 0:
            loads[6].wait()
            loads[7].wait()
        state = over_set(feed, which, state)
    factor = row_factor(state[0])
    gate, up = state[1] * factor, state[2] * factor
    hbuf[low, z] = (gate / (1.0 + jnp.exp(-gate)) * up).astype(BF16)
    out_ref[...] = (mid.astype(F32) + product(hbuf, 5, loads[8], wd)).astype(BF16)

    finish_sends(xbuf, 0)
    finish_sends(qbuf, 1)

    @pl.loop(1, n)
    def _(i):
        part_copy(lax.rem(me + i, n), 0).wait_send()

    finish_sends(abuf, 3)
    finish_sends(mbuf, 4)
    finish_sends(hbuf, 5)


def angle_tables(positions, device, key_width, head_dim):
    lane = jnp.arange(2 * head_dim, dtype=jnp.int32)
    second = lane >= head_dim
    col = jnp.where(second, lane + device * key_width, lane) % head_dim
    frequency = jnp.exp(
        -((col - col % 2).astype(F32) / head_dim) * jnp.log(jnp.float32(ROPE_BASE))
    )
    turned = ~second | (lane < head_dim + key_width)
    angles = positions.astype(F32)[:, None] * jnp.where(turned, frequency, 0.0)[None, :]
    sign = jnp.where(lane % 2 == 0, -1.0, 1.0)
    cosine, sine = jnp.cos(angles), jnp.sin(angles) * sign[None, :]
    return jnp.stack(
        [cosine[:, :head_dim], sine[:, :head_dim], cosine[:, head_dim:], sine[:, head_dim:]]
    )


def shards(
    hidden_in,
    attn_gain,
    w_query,
    w_key,
    w_value,
    rotated_prefix_keys,
    cache_values,
    w_out,
    ffn_gain,
    w_gate,
    w_up,
    w_down,
    doc_offsets,
    slot_request,
):
    n = lax.axis_size("ctx")
    device = lax.axis_index("ctx")
    rows, width = hidden_in.shape
    span, kv_heads, head_dim = rotated_prefix_keys.shape
    q_width, k_width = w_query.shape[1], w_key.shape[1]
    ff_width = w_gate.shape[1]
    slot_index = jnp.arange(rows, dtype=jnp.int32)
    positions = jnp.sum(
        jnp.where(slot_request[:, None] == slot_index[None, :], doc_offsets[None, :], 0), axis=1
    )
    tables = angle_tables(positions, device, k_width, head_dim)
    place = jnp.broadcast_to(positions[:, None], (rows, head_dim))
    own_heads = q_width // head_dim
    vmem = pl.BlockSpec(memory_space=pltpu.VMEM)
    hbm = pl.BlockSpec(memory_space=pl.ANY)
    weight_shapes = [
        (n, width, q_width),
        (2 * k_width, width * n),
        (kv_heads, span, head_dim),
        (kv_heads, span, head_dim),
        (n, q_width, width),
        (n, width, ff_width),
        (n, width, ff_width),
        (n, ff_width, width),
    ]
    block_shapes = [
        (4, n // 4, rows, width),
        (4, n // 4, rows, q_width + head_dim),
        (n, (own_heads + 1) * rows, head_dim),
        (n, (own_heads + 1) * rows, head_dim),
        (4, n // 4, rows, q_width),
        (4, n // 4, rows, width),
        (4, n // 4, rows, ff_width),
    ]
    return pl.pallas_call(
        functools.partial(layer_kernel, n),
        out_shape=jax.ShapeDtypeStruct((rows, width), BF16),
        in_specs=[vmem] * 5 + [hbm] * 9,
        out_specs=vmem,
        scratch_shapes=[pltpu.VMEM(shape, BF16) for shape in weight_shapes + block_shapes]
        + [
            pltpu.SemaphoreType.DMA((9,)),
            pltpu.SemaphoreType.DMA((6, n)),
            pltpu.SemaphoreType.DMA((6, n)),
        ],
        compiler_params=pltpu.CompilerParams(
            collective_id=0, has_side_effects=True, vmem_limit_bytes=62 * 1024 * 1024
        ),
        name="layer",
    )(
        hidden_in,
        attn_gain.reshape(n, 1, width),
        ffn_gain.reshape(n, 1, width),
        tables,
        place,
        w_query.reshape(n, width, q_width),
        w_key.T,
        w_value.T,
        jnp.transpose(rotated_prefix_keys, (1, 0, 2)),
        jnp.transpose(cache_values, (1, 0, 2)),
        w_out.reshape(n, q_width, width),
        w_gate.reshape(n, width, ff_width),
        w_up.reshape(n, width, ff_width),
        w_down.reshape(n, ff_width, width),
    )


def pick(*arrays):
    n = lax.axis_size("ctx")
    rows, width = arrays[0].shape
    span, kv_heads, head_dim = arrays[5].shape
    q_width, k_width, ff_width = arrays[2].shape[1], arrays[3].shape[1], arrays[9].shape[1]
    whole_tiles = (
        n % 4 == 0
        and n >= 8
        and head_dim == 128
        and rows % 16 == 0
        and all(w % 128 == 0 for w in (width, q_width, ff_width, span))
        and k_width % 16 == 0
        and 2 * k_width <= head_dim
        and head_dim % k_width == 0
    )
    if not whole_tiles:
        return plain_shards(*arrays)
    own_heads = q_width // head_dim
    group = own_heads * n // kv_heads
    if group % own_heads or own_heads > 8:
        return plain_shards(*arrays)
    return shards(*arrays)


def solution(mesh):
    return jax.shard_map(
        pick,
        mesh=mesh,
        in_specs=(
            P("groups", "ctx"),
            P(),
            P(None, "ctx"),
            P(None, "ctx"),
            P(None, "ctx"),
            P(("groups", "ctx"), None, None),
            P(("groups", "ctx"), None, None),
            P(None, "ctx"),
            P(),
            P(None, "ctx"),
            P(None, "ctx"),
            P(None, "ctx"),
            P("groups"),
            P("groups"),
        ),
        out_specs=P("groups", "ctx"),
        check_vma=False,
    )
```

```python
import functools
import math

import jax
import jax.numpy as jnp
from jax import lax
from jax.experimental import pallas as pl
from jax.experimental.pallas import tpu as pltpu
from jax.sharding import PartitionSpec as P

NORM_EPSILON = 1e-05
ROPE_BASE = 500000.0
MASKED = -1e30


def joined(part, axis, combine):
    gathered = jax.tree.map(lambda a: lax.all_gather(a, axis), part)

    def take(source):
        return jax.tree.map(lambda a: lax.dynamic_index_in_dim(a, source, 0, False), gathered)

    return lax.fori_loop(
        1, lax.axis_size(axis), lambda source, state: combine(state, take(source)), take(0)
    )


def rms_norm(values, gain_row):
    wide_rows = values.astype(jnp.float32)
    factor = lax.rsqrt(jnp.mean(wide_rows * wide_rows, axis=1, keepdims=True) + NORM_EPSILON)
    return (wide_rows * factor * gain_row[None, :]).astype(jnp.bfloat16)


def rotate(columns, first_col, positions, head_dim):
    col_count = columns.shape[1]
    pair_cols = first_col + jnp.arange(col_count // 2, dtype=jnp.int32) * 2
    in_head = (pair_cols % head_dim).astype(jnp.float32)
    frequency = jnp.exp(-(in_head / head_dim) * jnp.log(jnp.float32(ROPE_BASE)))
    angles = positions.astype(jnp.float32)[:, None] * frequency[None, :]
    paired = columns.reshape(columns.shape[0], col_count // 2, 2)
    even_part = paired[..., 0]
    odd_part = paired[..., 1]
    cosine = jnp.cos(angles)
    sine = jnp.sin(angles)
    turned = jnp.stack(
        [even_part * cosine - odd_part * sine, even_part * sine + odd_part * cosine], axis=-1
    )
    return turned.reshape(columns.shape)


def combine_parts(first_part, second_part):
    top_first, total_first, accum_first = first_part
    top_second, total_second, accum_second = second_part
    peak_score = jnp.maximum(top_first, top_second)
    share_first = jnp.exp(top_first - peak_score)
    share_second = jnp.exp(top_second - peak_score)
    merged_total = total_first * share_first + total_second * share_second
    merged_accum = accum_first * share_first[..., None] + accum_second * share_second[..., None]
    return (peak_score, merged_total, merged_accum)


def plain_shards(
    hidden_in,
    attn_gain,
    w_query,
    w_key,
    w_value,
    rotated_prefix_keys,
    cache_values,
    w_out,
    ffn_gain,
    w_gate,
    w_up,
    w_down,
    doc_offsets,
    slot_request,
):
    devices = lax.axis_size("ctx")
    device = lax.axis_index("ctx")
    batch_rows = hidden_in.shape[0]
    block_span, value_heads, head_dim = rotated_prefix_keys.shape
    query_width = w_query.shape[1]
    key_width = w_key.shape[1]
    head_count = query_width * devices // head_dim
    group_size = head_count // value_heads
    logit_scale_factor = 1.0 / math.sqrt(head_dim)
    slot_index = jnp.arange(batch_rows, dtype=jnp.int32)
    positions = jnp.sum(
        jnp.where(slot_request[:, None] == slot_index[None, :], doc_offsets[None, :], 0), axis=1
    )
    full_rows = lax.all_gather(hidden_in, "ctx", axis=1, tiled=True)
    normed = rms_norm(full_rows, attn_gain)
    query_part = rotate(
        jnp.dot(normed, w_query, preferred_element_type=jnp.float32),
        device * query_width,
        positions,
        head_dim,
    ).astype(jnp.bfloat16)
    key_part = rotate(
        jnp.dot(normed, w_key, preferred_element_type=jnp.float32),
        device * key_width,
        positions,
        head_dim,
    ).astype(jnp.bfloat16)
    value_part = jnp.dot(normed, w_value, preferred_element_type=jnp.float32).astype(jnp.bfloat16)
    queries, key_new, value_new = (
        lax.all_gather(query_part, "ctx", axis=1, tiled=True),
        lax.all_gather(key_part, "ctx", axis=1, tiled=True),
        lax.all_gather(value_part, "ctx", axis=1, tiled=True),
    )
    query_groups = queries.reshape(batch_rows, value_heads, group_size, head_dim)
    attention_logits = (
        jnp.einsum(
            "owqa,zwa->owqz", query_groups, rotated_prefix_keys, preferred_element_type=jnp.float32
        )
        * logit_scale_factor
    )
    places = device * block_span + jnp.arange(block_span, dtype=jnp.int32)
    visible = (places[None, :] < positions[:, None])[:, None, None, :]
    masked = jnp.where(visible, attention_logits, MASKED)
    block_top = jnp.max(masked, axis=3)
    weights = jnp.where(visible, jnp.exp(masked - block_top[..., None]), 0.0)
    block_total = jnp.sum(weights, axis=3)
    block_value_sum = jnp.einsum(
        "nelw,weh->nelh",
        weights.astype(jnp.bfloat16),
        cache_values,
        preferred_element_type=jnp.float32,
    )
    own_score = (
        jnp.einsum(
            "rkgd,rkd->rkg",
            query_groups,
            key_new.reshape(batch_rows, value_heads, head_dim),
            preferred_element_type=jnp.float32,
        )
        * logit_scale_factor
    ).reshape(batch_rows, head_count)
    spread_value = jnp.broadcast_to(
        value_new.reshape(batch_rows, value_heads, 1, head_dim),
        (batch_rows, value_heads, group_size, head_dim),
    ).reshape(batch_rows, head_count * head_dim)
    global_top, global_total, prefix_accum = joined(
        (block_top, block_total, block_value_sum), "ctx", combine_parts
    )
    finish_global_top = global_top
    finish_global_total = global_total
    finish_global_top = finish_global_top.reshape(batch_rows, head_count)
    finish_global_total = finish_global_total.reshape(batch_rows, head_count)
    peak_score = jnp.maximum(finish_global_top, own_score)
    kept_share = jnp.exp(finish_global_top - peak_score)
    fresh_share = jnp.exp(own_score - peak_score)
    denominator = finish_global_total * kept_share + fresh_share

    def columns(per_head):
        return jnp.repeat(per_head, head_dim, axis=1)

    value_cols = spread_value.astype(jnp.float32)
    attn_all = (
        (
            prefix_accum.reshape(batch_rows, head_count * head_dim) * columns(kept_share)
            + columns(fresh_share) * value_cols
        )
        / columns(denominator)
    ).astype(jnp.bfloat16)
    attn_part = jnp.dot(attn_all, w_out, preferred_element_type=jnp.float32)
    mid_part = (hidden_in.astype(jnp.float32) + attn_part).astype(jnp.bfloat16)
    mid_full = lax.all_gather(mid_part, "ctx", axis=1, tiled=True)
    normed_mid = rms_norm(mid_full, ffn_gain)
    gate_act = jnp.dot(normed_mid, w_gate, preferred_element_type=jnp.float32)
    up_act = jnp.dot(normed_mid, w_up, preferred_element_type=jnp.float32)
    hidden = (jax.nn.silu(gate_act) * up_act).astype(jnp.bfloat16)
    down_part = jnp.dot(
        lax.all_gather(hidden, "ctx", axis=1, tiled=True),
        w_down,
        preferred_element_type=jnp.float32,
    )
    return (mid_part.astype(jnp.float32) + down_part).astype(jnp.bfloat16)


MESH = pl.DeviceIdType.MESH
F32 = jnp.float32
BF16 = jnp.bfloat16


def dot(a, b):
    return jnp.dot(a, b, preferred_element_type=F32)


def dot_nt(a, b):
    return lax.dot_general(a, b, (((1,), (1,)), ((), ())), preferred_element_type=F32)


def turn(x, cosine, signed_sine):
    lane = lax.broadcasted_iota(jnp.int32, x.shape, 1)
    after = pltpu.roll(x, x.shape[1] - 1, 1)
    before = pltpu.roll(x, 1, 1)
    return x * cosine + jnp.where(lane % 2 == 0, after, before) * signed_sine


def three_terms(x):
    high = x.astype(BF16).astype(F32)
    left = x - high
    mid = left.astype(BF16).astype(F32)
    return high, mid, left - mid


def layer_kernel(
    n,
    hidden_ref,
    again_ref,
    fgain_ref,
    table_ref,
    place_ref,
    wq_hbm,
    wk_hbm,
    wv_hbm,
    keys_hbm,
    values_hbm,
    wo_hbm,
    wg_hbm,
    wu_hbm,
    wd_hbm,
    out_ref,
    wq,
    wkv,
    keys,
    values,
    wo,
    wg,
    wu,
    wd,
    xbuf,
    qbuf,
    asend,
    arecv,
    abuf,
    mbuf,
    hbuf,
    local_sem,
    send_sem,
    recv_sem,
):
    me = lax.axis_index("ctx")
    rows = hidden_ref.shape[0]
    kv_heads, span, head_dim = keys.shape
    q_width = wq.shape[2]
    k_width = wk_hbm.shape[0]
    own_heads = q_width // head_dim
    head_count = own_heads * n
    group = head_count // kv_heads
    stat_lanes = head_dim // own_heads
    scale = 1.0 / math.sqrt(head_dim)

    loads = [
        pltpu.make_async_copy(source, target, local_sem.at[i])
        for i, (source, target) in enumerate(
            [
                (wq_hbm, wq),
                (wk_hbm, wkv.at[pl.ds(0, k_width)]),
                (wv_hbm, wkv.at[pl.ds(k_width, k_width)]),
                (keys_hbm, keys),
                (values_hbm, values),
                (wo_hbm, wo),
                (wg_hbm, wg),
                (wu_hbm, wu),
                (wd_hbm, wd),
            ]
        )
    ]
    for load in loads:
        load.start()

    barrier = pltpu.get_barrier_semaphore()

    @pl.loop(1, n)
    def _(i):
        pl.semaphore_signal(
            barrier, inc=1, device_id={"ctx": lax.rem(me + i, n)}, device_id_type=MESH
        )

    low, z, z_steps = me % 4, me // 4, n // 4
    xbuf[low, z] = hidden_ref[...]
    pl.semaphore_wait(barrier, n - 1)

    other_core = me + 1 - 2 * (me % 2)
    other_y = me + 2 - 4 * ((me // 2) % 2)
    other_both = other_y + 1 - 2 * (other_y % 2)

    def block_copy(buf, phase, which, from_z, target, k):
        return pltpu.make_async_remote_copy(
            src_ref=buf.at[which, from_z],
            dst_ref=buf.at[which, from_z],
            send_sem=send_sem.at[phase, k],
            recv_sem=recv_sem.at[phase, from_z * 4 + which],
            device_id={"ctx": target},
            device_id_type=MESH,
        )

    def gather(buf, phase):
        plane = (other_both, other_y, other_core)
        for i in range(1, z_steps):
            block_copy(buf, phase, low, z, lax.rem(me + 4 * i, n), i - 1).start()
        k = z_steps - 1
        for i in range(z_steps):
            from_z = lax.rem(z + i, z_steps)
            if i:
                block_copy(buf, phase, low, from_z, other_core, 0).wait_recv()
            for peer in plane:
                block_copy(buf, phase, low, from_z, peer, k).start()
                k += 1
        yield low
        for peer in (other_core, other_y, other_both):
            which = peer % 4
            for i in range(z_steps):
                block_copy(buf, phase, which, lax.rem(z + i, z_steps), other_core, 0).wait_recv()
            yield which

    def gather_all(buf, phase):
        for _ in gather(buf, phase):
            pass

    def finish_sends(buf, phase):
        @pl.loop(0, n - 1)
        def _(k):
            block_copy(buf, phase, low, z, other_core, k).wait_send()

    def over_set(step, which, state):
        return lax.fori_loop(
            0, z_steps, lambda at_z, state: step(which, at_z, at_z * 4 + which, state), state,
            unroll=True,
        )

    def row_factor(squares):
        mean = jnp.sum(squares, axis=1, keepdims=True) / (squares.shape[1] * n)
        return lax.rsqrt(mean + NORM_EPSILON)

    def product(buf, phase, load, weight):
        def add(which, at_z, source, total):
            return total + dot(buf[which, at_z], weight[source])

        total = jnp.zeros((rows, weight.shape[2]), F32)
        for step, which in enumerate(gather(buf, phase)):
            if step == 0:
                load.wait()
            total = over_set(add, which, total)
        return total

    width = xbuf.shape[3]

    def project_in(which, at_z, source, state):
        squares, q_part, kv_part = state
        x = xbuf[which, at_z].astype(F32)
        scaled = (x * again_ref[source]).astype(BF16)
        cols = pl.ds(pl.multiple_of(source * width, width), width)
        return (
            squares + x * x,
            q_part + dot(scaled, wq[source]),
            kv_part + dot_nt(scaled, wkv[:, cols]),
        )

    state = tuple(jnp.zeros((rows, w), F32) for w in (width, q_width, 2 * k_width))
    for step, which in enumerate(gather(xbuf, 0)):
        if step == 0:
            for load in loads[:3]:
                load.wait()
        state = over_set(project_in, which, state)
    factor = row_factor(state[0])
    q_part, kv_part = state[1] * factor, state[2] * factor
    cosine, sine = table_ref[0], table_ref[1]
    for h in range(own_heads):
        cols = slice(h * head_dim, (h + 1) * head_dim)
        qbuf[low, z, :, cols] = turn(q_part[:, cols], cosine, sine).astype(BF16)
    kv_part = jnp.concatenate(
        [kv_part, jnp.zeros((rows, head_dim - 2 * k_width), F32)], axis=1
    )
    qbuf[low, z, :, q_width:] = turn(kv_part, table_ref[2], table_ref[3]).astype(BF16)
    gather_all(qbuf, 1)

    loads[3].wait()
    loads[4].wait()
    lane = lax.broadcasted_iota(jnp.int32, (rows, head_dim), 1)
    place = place_ref[...]
    limit = jnp.concatenate([place] * group, axis=0)[:, 0:1]
    at = me * span + lax.broadcasted_iota(jnp.int32, (group * rows, span), 1)
    visible = at < limit

    def part_copy(target, source):
        return pltpu.make_async_remote_copy(
            src_ref=asend.at[target],
            dst_ref=arecv.at[source],
            send_sem=send_sem.at[2, target],
            recv_sem=recv_sem.at[2, source],
            device_id={"ctx": target},
            device_id_type=MESH,
        )

    for g in range(kv_heads):
        query = jnp.concatenate(
            [
                qbuf[d % 4, d // 4, :, h * head_dim : (h + 1) * head_dim]
                for d in range(g * group // own_heads, (g + 1) * group // own_heads)
                for h in range(own_heads)
            ],
            axis=0,
        )
        logits = jnp.where(visible, dot_nt(query, keys[g]) * scale, MASKED)
        top = jnp.max(logits, axis=1, keepdims=True)
        weights = jnp.where(visible, jnp.exp(logits - top), 0.0)
        total = jnp.sum(weights, axis=1, keepdims=True)
        accum = dot(weights.astype(BF16), values[g]).astype(BF16)
        terms = three_terms(top) + three_terms(total)
        for d in range(group // own_heads):
            target = g * (group // own_heads) + d
            stats = jnp.zeros((rows, head_dim), F32)
            for h in range(own_heads):
                j = d * own_heads + h
                these = slice(j * rows, (j + 1) * rows)
                asend[target, h * rows : (h + 1) * rows, :] = accum[these]
                for t, term in enumerate(terms):
                    stats = jnp.where(lane == h * stat_lanes + t, term[these], stats)
            asend[target, own_heads * rows :, :] = stats.astype(BF16)

            @pl.when(me != target)
            def _():
                part_copy(target, me).start()

    arecv[me] = asend[me]

    @pl.loop(1, n)
    def _(i):
        part_copy(0, lax.rem(me + i, n)).wait_recv()

    def stats_of(s):
        x = arecv[s, own_heads * rows :, :].astype(F32)
        return x + pltpu.roll(x, head_dim - 1, 1) + pltpu.roll(x, head_dim - 2, 1)

    tops = lax.fori_loop(
        1, n, lambda s, top: jnp.maximum(top, stats_of(s)), stats_of(0), unroll=5
    )

    def merge(s, state):
        stats = stats_of(s)
        share = jnp.exp(stats - tops)
        total = state[0] + pltpu.roll(stats, head_dim - 3, 1) * share
        accums = tuple(
            state[1 + h]
            + arecv[s, h * rows : (h + 1) * rows, :].astype(F32)
            * share[:, h * stat_lanes : h * stat_lanes + 1]
            for h in range(own_heads)
        )
        return (total, *accums)

    zero = jnp.zeros((rows, head_dim), F32)
    totals, *accums = lax.fori_loop(0, n, merge, (zero,) * (1 + own_heads), unroll=4)

    pieces = head_dim // k_width
    first_piece = (me * own_heads // group) * pieces
    key_new, value_new = zero, zero
    for i in range(pieces):
        source = first_piece + i
        piece = qbuf[source % 4, source // 4, :, q_width:].astype(F32)
        key_piece = jnp.where(lane < k_width, piece, 0.0)
        value_piece = jnp.where((lane >= k_width) & (lane < 2 * k_width), piece, 0.0)
        key_new += pltpu.roll(key_piece, i * k_width, 1) if i else key_piece
        shift = (i * k_width - k_width) % head_dim
        value_new += pltpu.roll(value_piece, shift, 1) if shift else value_piece
    for h in range(own_heads):
        cols = slice(h * head_dim, (h + 1) * head_dim)
        at_stat = slice(h * stat_lanes, h * stat_lanes + 1)
        query = qbuf[low, z, :, cols].astype(F32)
        own_score = jnp.sum(query * key_new, axis=1, keepdims=True) * scale
        top = tops[:, at_stat]
        peak = jnp.maximum(top, own_score)
        kept, fresh = jnp.exp(top - peak), jnp.exp(own_score - peak)
        below = totals[:, at_stat] * kept + fresh
        abuf[low, z, :, cols] = ((accums[h] * kept + fresh * value_new) / below).astype(BF16)

    attn_part = product(abuf, 3, loads[5], wo)
    mid = (hidden_ref[...].astype(F32) + attn_part).astype(BF16)
    mbuf[low, z] = mid

    def feed(which, at_z, source, state):
        squares, gate, up = state
        x = mbuf[which, at_z].astype(F32)
        scaled = (x * fgain_ref[source]).astype(BF16)
        return (
            squares + x * x,
            gate + dot(scaled, wg[source]),
            up + dot(scaled, wu[source]),
        )

    ff_width = wg.shape[2]
    state = tuple(jnp.zeros((rows, w), F32) for w in (width, ff_width, ff_width))
    for step, which in enumerate(gather(mbuf, 4)):
        if step == 0:
            loads[6].wait()
            loads[7].wait()
        state = over_set(feed, which, state)
    factor = row_factor(state[0])
    gate, up = state[1] * factor, state[2] * factor
    hbuf[low, z] = (gate / (1.0 + jnp.exp(-gate)) * up).astype(BF16)
    out_ref[...] = (mid.astype(F32) + product(hbuf, 5, loads[8], wd)).astype(BF16)

    finish_sends(xbuf, 0)
    finish_sends(qbuf, 1)

    @pl.loop(1, n)
    def _(i):
        part_copy(lax.rem(me + i, n), 0).wait_send()

    finish_sends(abuf, 3)
    finish_sends(mbuf, 4)
    finish_sends(hbuf, 5)


def angle_tables(positions, device, key_width, head_dim):
    lane = jnp.arange(2 * head_dim, dtype=jnp.int32)
    second = lane >= head_dim
    col = jnp.where(second, lane + device * key_width, lane) % head_dim
    frequency = jnp.exp(
        -((col - col % 2).astype(F32) / head_dim) * jnp.log(jnp.float32(ROPE_BASE))
    )
    turned = ~second | (lane < head_dim + key_width)
    angles = positions.astype(F32)[:, None] * jnp.where(turned, frequency, 0.0)[None, :]
    sign = jnp.where(lane % 2 == 0, -1.0, 1.0)
    cosine, sine = jnp.cos(angles), jnp.sin(angles) * sign[None, :]
    return jnp.stack(
        [cosine[:, :head_dim], sine[:, :head_dim], cosine[:, head_dim:], sine[:, head_dim:]]
    )


def shards(
    hidden_in,
    attn_gain,
    w_query,
    w_key,
    w_value,
    rotated_prefix_keys,
    cache_values,
    w_out,
    ffn_gain,
    w_gate,
    w_up,
    w_down,
    doc_offsets,
    slot_request,
):
    n = lax.axis_size("ctx")
    device = lax.axis_index("ctx")
    rows, width = hidden_in.shape
    span, kv_heads, head_dim = rotated_prefix_keys.shape
    q_width, k_width = w_query.shape[1], w_key.shape[1]
    ff_width = w_gate.shape[1]
    slot_index = jnp.arange(rows, dtype=jnp.int32)
    positions = jnp.sum(
        jnp.where(slot_request[:, None] == slot_index[None, :], doc_offsets[None, :], 0), axis=1
    )
    tables = angle_tables(positions, device, k_width, head_dim)
    place = jnp.broadcast_to(positions[:, None], (rows, head_dim))
    own_heads = q_width // head_dim
    vmem = pl.BlockSpec(memory_space=pltpu.VMEM)
    hbm = pl.BlockSpec(memory_space=pl.ANY)
    weight_shapes = [
        (n, width, q_width),
        (2 * k_width, width * n),
        (kv_heads, span, head_dim),
        (kv_heads, span, head_dim),
        (n, q_width, width),
        (n, width, ff_width),
        (n, width, ff_width),
        (n, ff_width, width),
    ]
    block_shapes = [
        (4, n // 4, rows, width),
        (4, n // 4, rows, q_width + head_dim),
        (n, (own_heads + 1) * rows, head_dim),
        (n, (own_heads + 1) * rows, head_dim),
        (4, n // 4, rows, q_width),
        (4, n // 4, rows, width),
        (4, n // 4, rows, ff_width),
    ]
    return pl.pallas_call(
        functools.partial(layer_kernel, n),
        out_shape=jax.ShapeDtypeStruct((rows, width), BF16),
        in_specs=[vmem] * 5 + [hbm] * 9,
        out_specs=vmem,
        scratch_shapes=[pltpu.VMEM(shape, BF16) for shape in weight_shapes + block_shapes]
        + [
            pltpu.SemaphoreType.DMA((9,)),
            pltpu.SemaphoreType.DMA((6, n)),
            pltpu.SemaphoreType.DMA((6, n)),
        ],
        compiler_params=pltpu.CompilerParams(
            collective_id=0, has_side_effects=True, vmem_limit_bytes=62 * 1024 * 1024
        ),
        name="layer",
    )(
        hidden_in,
        attn_gain.reshape(n, 1, width),
        ffn_gain.reshape(n, 1, width),
        tables,
        place,
        w_query.reshape(n, width, q_width),
        w_key.T,
        w_value.T,
        jnp.transpose(rotated_prefix_keys, (1, 0, 2)),
        jnp.transpose(cache_values, (1, 0, 2)),
        w_out.reshape(n, q_width, width),
        w_gate.reshape(n, width, ff_width),
        w_up.reshape(n, width, ff_width),
        w_down.reshape(n, ff_width, width),
    )


def pick(*arrays):
    n = lax.axis_size("ctx")
    rows, width = arrays[0].shape
    span, kv_heads, head_dim = arrays[5].shape
    q_width, k_width, ff_width = arrays[2].shape[1], arrays[3].shape[1], arrays[9].shape[1]
    whole_tiles = (
        n % 4 == 0
        and n >= 8
        and head_dim == 128
        and rows % 16 == 0
        and all(w % 128 == 0 for w in (width, q_width, ff_width, span))
        and k_width % 16 == 0
        and 2 * k_width <= head_dim
        and head_dim % k_width == 0
    )
    if not whole_tiles:
        return plain_shards(*arrays)
    own_heads = q_width // head_dim
    group = own_heads * n // kv_heads
    if group % own_heads or own_heads > 8:
        return plain_shards(*arrays)
    return shards(*arrays)


def solution(mesh):
    return jax.shard_map(
        pick,
        mesh=mesh,
        in_specs=(
            P("groups", "ctx"),
            P(),
            P(None, "ctx"),
            P(None, "ctx"),
            P(None, "ctx"),
            P(("groups", "ctx"), None, None),
            P(("groups", "ctx"), None, None),
            P(None, "ctx"),
            P(),
            P(None, "ctx"),
            P(None, "ctx"),
            P(None, "ctx"),
            P("groups"),
            P("groups"),
        ),
        out_specs=P("groups", "ctx"),
        check_vma=False,
    )
```
